32 devices in a mesh: dp: 8 (over z, y), blk: 4 (over x, core).
Axes of the slice: x: 2, y: 2, z: 4, core: 2. Of those that a mesh axis runs over, the one named last changes fastest.
Arguments:
- grads: bfloat16 [8, 4, 1024, 1024], P('dp', None, None, 'blk'), may hold values from -4 to 4
- left_old: float32 [4, 1024, 1024], P('blk', 'dp'), may hold values from -0.3 to 0.3
- right_old: float32 [4, 1024, 1024], P('blk', 'dp'), may hold values from -0.3 to 0.3
- left_root: bfloat16 [4, 1024, 1024], P('blk'), may hold values from -0.1875 to 0.1875
- right_root: bfloat16 [4, 1024, 1024], P('blk'), may hold values from -0.1875 to 0.1875
Outputs:
- update: bfloat16 [4, 1024, 1024], P(None, 'dp', 'blk')
- left_stat: float32 [4, 1024, 1024], P('blk', 'dp')
- right_stat: float32 [4, 1024, 1024], P('blk', 'dp')
The draws below stay inside these ranges and needn't reach their ends.
All inputs are finite; a program needn't handle non-finite values.
Results may differ from the reference program's by a relative error of at most 0.0059.
Values may be sent and summed in bfloat16 or wider, within the bound.
No kernel may reach another device: no remote copies, remote signals or barrier semaphores. Data moves between devices by JAX's collectives and lax.ppermute only.
A program may use at most 64 MiB of HBM per device.

```python
import jax
import jax.numpy as jnp
from jax import lax

BLOCK = 1024
NB = 4
N_DP = 8


def raised(values, stream_key, source, target, parts, factor):
    owner, partner = [(jnp.arange(values.shape[dim]) // (values.shape[dim] // parts)).reshape([-1 if axis == dim else 1 for axis in range(values.ndim)]) for dim in (source, target)]
    chosen = jax.random.permutation(stream_key, parts)[partner]
    strong = (owner == chosen) | (owner == (partner + parts // 2) % parts)
    return jnp.where(strong, factor * values, values)


def level_of(own_key, shape, pieces, smallest, high):
    level, own = 1.0, jax.random.fold_in(own_key, 6)
    for dim, shards_of in pieces:
        draws = jnp.exp(jax.random.uniform(jax.random.fold_in(own, dim), (shards_of,), jnp.float32, smallest / len(pieces), high / len(pieces)))
        level = level * jnp.repeat(draws, shape[dim] // shards_of).reshape([-1 if axis == dim else 1 for axis in range(len(shape))])
    return level


def centred(rng, shape, deviation, bound, shards=(), kind=jnp.bfloat16):
    values = deviation * jax.random.normal(rng, shape, jnp.float32)
    if shards:
        values = values * level_of(rng, shape, shards, -0.22, 0.18)
    return jnp.clip(values, -bound, bound).astype(kind)


def bell_draw_with(key, shape, spread, most, cuts, heavy, held_as=jnp.bfloat16):
    values = spread * jax.random.normal(key, shape, jnp.float32)
    if cuts:
        values = values * level_of(key, shape, cuts, -0.22, 0.18)
    return jnp.clip(raised(values, jax.random.fold_in(key, 3), *heavy), -most, most).astype(held_as)


def setup_inputs(seed: int = 0) -> dict:
    splits = jax.random.split(jax.random.key(seed), 6)
    grads = bell_draw_with(splits[0], (N_DP, NB, BLOCK, BLOCK), 0.5, 4.0, ((0, 8), (3, 4)), (0, 2, 8, 2.0))
    left_old = centred(splits[1], (NB, BLOCK, BLOCK), 0.05, 0.3, ((0, 4), (1, 8)), jnp.float32)
    right_old = centred(splits[2], (NB, BLOCK, BLOCK), 0.05, 0.3, ((0, 4), (1, 8)), jnp.float32)
    left_root = centred(splits[3], (NB, BLOCK, BLOCK), BLOCK ** -0.5, 0.1875, ((0, 4),))
    right_root = centred(splits[4], (NB, BLOCK, BLOCK), BLOCK ** -0.5, 0.1875, ((0, 4),))
    return dict(grads=grads, left_old=left_old, right_old=right_old, left_root=left_root, right_root=right_root)


stat_decay = 0.9


def reference(grads, left_old, right_old, left_root, right_root):
    def accumulate(running, member):
        return running + member.astype(jnp.float32), None

    zeros_start = jnp.zeros(grads.shape[1:], jnp.float32)
    summed, _ = lax.scan(accumulate, zeros_start, grads)
    gradient = summed.astype(jnp.bfloat16)

    def one_block(items):
        grad_block, left_prev, right_prev, left_inv, right_inv = items
        left_prod = jnp.dot(grad_block, grad_block.T, preferred_element_type=jnp.float32)
        right_prod = jnp.dot(grad_block.T, grad_block, preferred_element_type=jnp.float32)
        stat_scale = (1.0 - stat_decay) / BLOCK
        left_new = stat_decay * left_prev + stat_scale * left_prod
        right_new = stat_decay * right_prev + stat_scale * right_prod
        half_done = jnp.dot(left_inv, grad_block, preferred_element_type=jnp.float32).astype(jnp.bfloat16)
        result = jnp.dot(half_done, right_inv, preferred_element_type=jnp.float32).astype(jnp.bfloat16)
        return result, left_new, right_new

    update, left_stat, right_stat = lax.map(one_block, (gradient, left_old, right_old, left_root, right_root))
    return (update, left_stat, right_stat)
```

```python
import jax
import jax.numpy as jnp
from jax import lax
from jax.sharding import PartitionSpec as P

stat_decay = 0.9
chunk_parts = (3, 3, 2)


def swap(values, axis, mask):
    size = lax.axis_size(axis)
    return lax.ppermute(values, axis, [(i, i ^ mask) for i in range(size)])


def pick(values, index, dim):
    return lax.dynamic_index_in_dim(values, index, dim, keepdims=False)


def ordered(pieces, index):
    count = len(pieces)
    return [
        lax.select_n(index, *[pieces[place ^ me] for me in range(count)])
        for place in range(count)
    ]


def chunks_of(rows):
    total = sum(chunk_parts)
    edges = [0]
    for part in chunk_parts:
        edges.append(edges[-1] + rows * part // total)
    return list(zip(edges[:-1], edges[1:]))


def on_device(grads, left_old, right_old, left_root, right_root):
    members, owners = lax.axis_size("dp"), lax.axis_size("blk")
    near = members // 2
    block_size = left_root.shape[-1]
    strip_rows = left_old.shape[1]
    dp_index = lax.axis_index("dp")
    blk_index = lax.axis_index("blk")
    low = dp_index % near
    depth = block_size // near
    cols = grads.shape[3]
    split = grads[0].reshape(owners, near, depth, cols)

    spans = chunks_of(depth)
    firsts = []
    for start, stop in spans:
        part = split[:, :, start:stop]
        firsts.append(
            [swap(pick(part, low ^ m, 1), "dp", m) for m in range(1, near)]
        )
    gathered = []
    for (start, stop), first in zip(spans, firsts):
        part = split[:, :, start:stop]
        near_sum = pick(part, low, 1).astype(jnp.float32)
        for piece in first:
            near_sum = near_sum + piece.astype(jnp.float32)
        far = swap(near_sum.astype(jnp.bfloat16), "dp", near)
        owned = (near_sum + far.astype(jnp.float32)).astype(jnp.bfloat16)
        pieces = [pick(owned, blk_index, 0)] + [
            swap(pick(owned, blk_index ^ m, 0), "blk", m) for m in range(1, owners)
        ]
        strip = jnp.concatenate(ordered(pieces, blk_index), axis=1)[None]
        mask = near // 2
        while mask:
            other = swap(strip, "dp", mask)
            strip = jnp.concatenate(ordered([strip, other], (low // mask) % 2), axis=0)
            mask //= 2
        gathered.append(strip)
    places = [0]
    mask = near // 2
    while mask:
        places = places + [p + mask for p in places]
        mask //= 2
    whole = jnp.concatenate(gathered, axis=1)
    order = [places.index(p) for p in range(near)]
    whole = jnp.concatenate([whole[i] for i in order], axis=0)

    own_rows = lax.dynamic_slice_in_dim(whole, dp_index * strip_rows, strip_rows, 0)
    own_columns = lax.dynamic_slice_in_dim(whole, dp_index * strip_rows, strip_rows, 1)
    root_rows = lax.dynamic_slice_in_dim(left_root[0], dp_index * strip_rows, strip_rows, 0)
    half_done = jnp.dot(root_rows, whole, preferred_element_type=jnp.float32).astype(jnp.bfloat16)
    owner_update = jnp.dot(half_done, right_root[0], preferred_element_type=jnp.float32).astype(
        jnp.bfloat16
    )
    by_columns = owner_update.reshape(strip_rows, owners, cols)
    back = [pick(by_columns, blk_index, 1)] + [
        swap(pick(by_columns, blk_index ^ m, 1), "blk", m) for m in range(1, owners)
    ]
    update = jnp.stack(ordered(back, blk_index))
    left_prod = jnp.einsum("ik,jk->ij", own_rows, whole, preferred_element_type=jnp.float32)
    right_prod = jnp.einsum("ki,kj->ij", own_columns, whole, preferred_element_type=jnp.float32)
    stat_scale = (1.0 - stat_decay) / block_size
    left_stat = stat_decay * left_old + stat_scale * left_prod
    right_stat = stat_decay * right_old + stat_scale * right_prod
    return (update, left_stat, right_stat)


def solution(mesh):
    placed = (
        P("dp", None, None, "blk"),
        P("blk", "dp", None),
        P("blk", "dp", None),
        P("blk", None, None),
        P("blk", None, None),
    )
    return jax.shard_map(
        on_device,
        mesh=mesh,
        in_specs=placed,
        out_specs=(P(None, "dp", "blk"), P("blk", "dp", None), P("blk", "dp", None)),
        check_vma=False,
    )
```

```python
import functools

import jax
import jax.numpy as jnp
from jax import lax
from jax.experimental import pallas as pl
from jax.experimental.pallas import tpu as pltpu
from jax.sharding import PartitionSpec as P

stat_decay = 0.9
chunk_parts = (1,1,1,1)
sum_ways = (1,)
gather_ways = (1, -1,)
vmem_bytes = 24 * 2**20


def swap(values, axis, mask):
    size = lax.axis_size(axis)
    return lax.ppermute(values, axis, [(i, i ^ mask) for i in range(size)])


def pick(values, index, dim):
    return lax.dynamic_index_in_dim(values, index, dim, keepdims=False)


def ordered(pieces, index):
    count = len(pieces)
    return [
        lax.select_n(index, *[pieces[place ^ me] for me in range(count)])
        for place in range(count)
    ]


def chunks_of(rows):
    total = sum(chunk_parts)
    edges = [0]
    for part in chunk_parts:
        edges.append(edges[-1] + rows * part // total)
    return list(zip(edges[:-1], edges[1:]))


def wave(count, stages):
    return [
        (k, s)
        for turn in range(count * 1 + stages)
        for k in reversed(range(count))
        for s in range(stages)
        if k * 1 + s == turn
    ]


def update_kernel(count, blk_ref, *refs):
    strips, (root_rows, right_root), outs, rows = refs[:count], refs[count : count + 2], refs[count + 2 : -1], refs[-1]
    total = None
    start = 0
    for strip in strips:
        stop = start + strip.shape[0]
        part = jnp.dot(
            root_rows[0, :, start:stop], strip[...], preferred_element_type=jnp.float32
        )
        total = part if total is None else total + part
        start = stop
    rows[...] = jnp.dot(
        total.astype(jnp.bfloat16), right_root[0], preferred_element_type=jnp.float32
    ).astype(jnp.bfloat16)
    width = outs[0].shape[1]
    for m, out in enumerate(outs):
        out[...] = rows[:, pl.ds(pl.multiple_of((blk_ref[1] ^ m) * width, width), width)]


def make_update(blk_index, dp_index, strips, left_root, right_root, strip_rows, owners, cols):
    block_size = left_root.shape[-1]
    whole = lambda shape: pl.BlockSpec(shape, lambda i, s: (0,) * len(shape))
    return pl.pallas_call(
        functools.partial(update_kernel, len(strips)),
        grid_spec=pltpu.PrefetchScalarGridSpec(
            num_scalar_prefetch=1,
            grid=(1,),
            in_specs=[whole(s.shape) for s in strips]
            + [
                pl.BlockSpec((1, strip_rows, block_size), lambda i, s: (0, s[0], 0)),
                whole(right_root.shape),
            ],
            out_specs=[whole((strip_rows, cols))] * owners,
            scratch_shapes=[pltpu.VMEM((strip_rows, block_size), jnp.bfloat16)],
        ),
        out_shape=[jax.ShapeDtypeStruct((strip_rows, cols), jnp.bfloat16)] * owners,
        compiler_params=pltpu.CompilerParams(vmem_limit_bytes=vmem_bytes),
        cost_estimate=pl.CostEstimate(flops=1000, bytes_accessed=1000, transcendentals=0),
    )(jnp.stack([dp_index, blk_index]).astype(jnp.int32), *strips, left_root, right_root)


def stat_kernel(count, dp_ref, *refs):
    strips, (left_old, right_old, left_new, right_new, whole) = refs[:count], refs[count:]
    start = 0
    for strip in strips:
        whole[start : start + strip.shape[0], :] = strip[...]
        start += strip.shape[0]
    rows = left_old.shape[1]
    scale = (1.0 - stat_decay) / whole.shape[0]
    place = pl.ds(pl.multiple_of(dp_ref[0] * rows, rows), rows)
    left_prod = lax.dot_general(
        whole[place, :], whole[...], (((1,), (1,)), ((), ())), preferred_element_type=jnp.float32
    )
    left_new[0] = stat_decay * left_old[0] + scale * left_prod
    right_prod = lax.dot_general(
        whole[:, place], whole[...], (((0,), (0,)), ((), ())), preferred_element_type=jnp.float32
    )
    right_new[0] = stat_decay * right_old[0] + scale * right_prod


def make_stats(dp_index, strips, left_old, right_old):
    block_size = left_old.shape[-1]
    same = [jax.ShapeDtypeStruct(left_old.shape, jnp.float32)] * 2
    vmem = pl.BlockSpec(memory_space=pltpu.VMEM)
    return pl.pallas_call(
        functools.partial(stat_kernel, len(strips)),
        in_specs=[pl.BlockSpec(memory_space=pltpu.SMEM)] + [vmem] * (len(strips) + 2),
        out_specs=[vmem] * 2,
        out_shape=same,
        scratch_shapes=[pltpu.VMEM((block_size, block_size), jnp.bfloat16)],
        compiler_params=pltpu.CompilerParams(vmem_limit_bytes=vmem_bytes),
        cost_estimate=pl.CostEstimate(flops=1000, bytes_accessed=1000, transcendentals=0),
    )(dp_index.astype(jnp.int32)[None], *strips, left_old, right_old)


def on_device(grads, left_old, right_old, left_root, right_root):
    members, owners = lax.axis_size("dp"), lax.axis_size("blk")
    near = members // 2
    bits = near.bit_length() - 1
    block_size = left_root.shape[-1]
    strip_rows = left_old.shape[1]
    dp_index = lax.axis_index("dp")
    blk_index = lax.axis_index("blk")
    place = [(dp_index >> j) & 1 for j in range(bits)]
    cols = grads.shape[3]
    spans = chunks_of(block_size)
    state = {}
    last = [None]

    def after(values):
        if last[0] is None:
            return values
        return lax.optimization_barrier((values, last[0]))[0]

    def dim_of(j, taken):
        return 1 + len([i for i in range(bits) if i > j and i not in taken])

    def send(k, s, values):
        with jax.named_scope(f"R{s}c{k}m0"):
            return swap(values, "dp", 1 << rs_order(k)[s])

    def rs_order(k):
        return list(range(bits))[:: sum_ways[k % len(sum_ways)]]

    def ag_order(k):
        return list(range(bits))[:: gather_ways[k % len(gather_ways)]]

    def part_of(k, j, index):
        start, stop = spans[k]
        high, depth = 2 ** (bits - 1 - j), (stop - start) // near
        low = 2**j * depth
        rows = grads[0, :, start:stop].reshape(owners, high, 2, low, cols)
        rows = lax.dynamic_slice_in_dim(rows, index, 1, 2)
        return rows.reshape(owners, *([2] * (bits - 1)), depth, cols)

    def first(k):
        j = rs_order(k)[0]
        state[k] = send(k, 0, part_of(k, j, 1 - place[j]))

    def step(k, s):
        order = rs_order(k)
        if s < bits:
            if s == 0:
                own, received = part_of(k, order[0], place[order[0]]), after(state[k])
            else:
                own, received = state[k]
                received = after(received)
                own = pick(own, place[order[s]], dim_of(order[s], order[:s]))
            total = own.astype(jnp.float32) + received.astype(jnp.float32)
            if s + 1 < bits:
                j = order[s + 1]
                sent = pick(total, 1 - place[j], dim_of(j, order[: s + 1])).astype(jnp.bfloat16)
                state[k] = (total, send(k, s + 1, sent))
            else:
                sent = total.astype(jnp.bfloat16)
                with jax.named_scope(f"Z{k}m0"):
                    state[k] = (total, swap(sent, "dp", near))
            last[0] = sent
        elif s == bits:
            total, far = state[k]
            far = after(far)
            owned = (total + far.astype(jnp.float32)).astype(jnp.bfloat16)
            state[k] = [pick(owned, blk_index, 0)]
            for m in range(1, owners):
                with jax.named_scope(f"B{k}m{m}"):
                    state[k].append(swap(pick(owned, blk_index ^ m, 0), "blk", m))
            last[0] = owned
        else:
            g = s - bits - 1
            if g == 0:
                pieces = after(state[k])
                strip = jnp.concatenate(ordered(pieces, blk_index), axis=1)[None]
            else:
                strip, other = state[k]
                other = after(other)
                j = ag_order(k)[g - 1]
                strip = jnp.concatenate(ordered([strip, other], place[j]), axis=0)
            last[0] = strip
            if g < bits:
                with jax.named_scope(f"A{g}c{k}m0"):
                    state[k] = (strip, swap(strip, "dp", 1 << ag_order(k)[g]))
            else:
                state[k] = strip

    order = [] or wave(len(spans), 2 * bits + 2)
    for k in range(len(spans)):
        first(k)
    for k, s in order:
        step(k, s)
    strips = []
    for k in range(len(spans)):
        places = [0]
        for j in ag_order(k):
            places = places + [p + (1 << j) for p in places]
        strip = state[k]
        if places != list(range(near)):
            strip = jnp.concatenate([strip[places.index(p)][None] for p in range(near)], axis=0)
        strips.append(strip.reshape(-1, block_size))

    aligned = cols % 128 == 0 and strip_rows % 128 == 0
    if aligned:
        back = list(make_update(blk_index, dp_index, strips, left_root, right_root, strip_rows, owners, cols))
    else:
        whole = jnp.concatenate(strips, axis=0)
        root_rows = lax.dynamic_slice_in_dim(left_root[0], dp_index * strip_rows, strip_rows, 0)
        half_done = jnp.dot(root_rows, whole, preferred_element_type=jnp.float32)
        full = jnp.dot(
            half_done.astype(jnp.bfloat16), right_root[0], preferred_element_type=jnp.float32
        )
        by_columns = full.astype(jnp.bfloat16).reshape(strip_rows, owners, cols)
        back = [pick(by_columns, blk_index ^ m, 1) for m in range(owners)]
    for m in range(1, owners):
        with jax.named_scope(f"U0m{m}"):
            back[m] = swap(back[m], "blk", m)
    if aligned:
        left_stat, right_stat = make_stats(dp_index, strips, left_old, right_old)
    else:
        own_rows = lax.dynamic_slice_in_dim(whole, dp_index * strip_rows, strip_rows, 0)
        own_columns = lax.dynamic_slice_in_dim(whole, dp_index * strip_rows, strip_rows, 1)
        left_prod = jnp.einsum("ik,jk->ij", own_rows, whole, preferred_element_type=jnp.float32)
        right_prod = jnp.einsum("ki,kj->ij", own_columns, whole, preferred_element_type=jnp.float32)
        stat_scale = (1.0 - stat_decay) / block_size
        left_stat = stat_decay * left_old + stat_scale * left_prod
        right_stat = stat_decay * right_old + stat_scale * right_prod
    update = jnp.stack(ordered(back, blk_index))
    return (update, left_stat, right_stat)


def solution(mesh):
    placed = (
        P("dp", None, None, "blk"),
        P("blk", "dp", None),
        P("blk", "dp", None),
        P("blk", None, None),
        P("blk", None, None),
    )
    return jax.shard_map(
        on_device,
        mesh=mesh,
        in_specs=placed,
        out_specs=(P(None, "dp", "blk"), P("blk", "dp", None), P("blk", "dp", None)),
        check_vma=False,
    )
```

```python
import functools

import jax
import jax.numpy as jnp
from jax import lax
from jax.experimental import pallas as pl
from jax.experimental.pallas import tpu as pltpu
from jax.sharding import PartitionSpec as P

stat_decay = 0.9
chunk_parts = (1, 1, 1, 1)
sum_ways = (1,)
gather_ways = (1, -1, 1, -1,)
groups = ((0,), (1,), (2,), (3,))
steps = (
    "s00", "s10", "s01", "s20", "s11", "s30", "s21", "s02", "g00", "s31",
    "s12", "g01", "g10", "s22", "g20", "g11", "s32", "g30", "g02", "g21",
    "g31", "g12", "g22", "g03", "g32", "g13", "g23", "g33",
)
vmem_bytes = 24 * 2**20


def swap(values, axis, mask):
    size = lax.axis_size(axis)
    return lax.ppermute(values, axis, [(i, i ^ mask) for i in range(size)])


def pick(values, index, dim):
    return lax.dynamic_index_in_dim(values, index, dim, keepdims=False)


def ordered(pieces, index):
    count = len(pieces)
    return [
        lax.select_n(index, *[pieces[place ^ me] for me in range(count)])
        for place in range(count)
    ]


def chunks_of(rows):
    total = sum(chunk_parts)
    edges = [0]
    for part in chunk_parts:
        edges.append(edges[-1] + rows * part // total)
    return list(zip(edges[:-1], edges[1:]))


def steps_of(bits):
    if bits == 2:
        return [(name[0], int(name[1]), int(name[2])) for name in steps]
    stage_of = lambda given, k: (bits if given[k % len(given)] else 1) + 1
    sums = [("s", k, s) for k in range(len(chunk_parts)) for s in range(stage_of(sum_ways, k))]
    sums.sort(key=lambda step: (step[1] + step[2], -step[1]))
    gathers = [("g", g, s) for g in range(len(groups)) for s in range(stage_of(gather_ways, g) + 1)]
    return sums + sorted(gathers, key=lambda step: (step[1] + step[2], -step[1]))


def hold(values, earlier):
    anywhere = pl.BlockSpec(memory_space=pl.ANY)
    return pl.pallas_call(
        lambda *refs: None,
        in_specs=[anywhere, anywhere],
        out_specs=anywhere,
        out_shape=jax.ShapeDtypeStruct(values.shape, values.dtype),
        input_output_aliases={0: 0},
        compiler_params=pltpu.CompilerParams(vmem_limit_bytes=2**20),
        cost_estimate=pl.CostEstimate(flops=1000, bytes_accessed=1000, transcendentals=0),
    )(values, earlier)


def update_kernel(count, blk_ref, *refs):
    strips, (root_rows, right_root), outs, rows = refs[:count], refs[count : count + 2], refs[count + 2 : -1], refs[-1]
    total = None
    start = 0
    for strip in strips:
        stop = start + strip.shape[0]
        part = jnp.dot(
            root_rows[0, :, start:stop], strip[...], preferred_element_type=jnp.float32
        )
        total = part if total is None else total + part
        start = stop
    rows[...] = jnp.dot(
        total.astype(jnp.bfloat16), right_root[0], preferred_element_type=jnp.float32
    ).astype(jnp.bfloat16)
    width = outs[0].shape[1]
    for m, out in enumerate(outs):
        out[...] = rows[:, pl.ds(pl.multiple_of((blk_ref[1] ^ m) * width, width), width)]


def make_update(blk_index, dp_index, strips, left_root, right_root, strip_rows, owners, cols):
    block_size = left_root.shape[-1]
    whole = lambda shape: pl.BlockSpec(shape, lambda i, s: (0,) * len(shape))
    return pl.pallas_call(
        functools.partial(update_kernel, len(strips)),
        grid_spec=pltpu.PrefetchScalarGridSpec(
            num_scalar_prefetch=1,
            grid=(1,),
            in_specs=[whole(s.shape) for s in strips]
            + [
                pl.BlockSpec((1, strip_rows, block_size), lambda i, s: (0, s[0], 0)),
                whole(right_root.shape),
            ],
            out_specs=[whole((strip_rows, cols))] * owners,
            scratch_shapes=[pltpu.VMEM((strip_rows, block_size), jnp.bfloat16)],
        ),
        out_shape=[jax.ShapeDtypeStruct((strip_rows, cols), jnp.bfloat16)] * owners,
        compiler_params=pltpu.CompilerParams(vmem_limit_bytes=vmem_bytes),
        cost_estimate=pl.CostEstimate(flops=1000, bytes_accessed=1000, transcendentals=0),
    )(jnp.stack([dp_index, blk_index]).astype(jnp.int32), *strips, left_root, right_root)


def stat_kernel(count, dp_ref, *refs):
    strips, (left_old, right_old, left_new, right_new, whole) = refs[:count], refs[count:]
    start = 0
    for strip in strips:
        whole[start : start + strip.shape[0], :] = strip[...]
        start += strip.shape[0]
    rows = left_old.shape[1]
    scale = (1.0 - stat_decay) / whole.shape[0]
    place = pl.ds(pl.multiple_of(dp_ref[0] * rows, rows), rows)
    left_prod = lax.dot_general(
        whole[place, :], whole[...], (((1,), (1,)), ((), ())), preferred_element_type=jnp.float32
    )
    left_new[0] = stat_decay * left_old[0] + scale * left_prod
    right_prod = lax.dot_general(
        whole[:, place], whole[...], (((0,), (0,)), ((), ())), preferred_element_type=jnp.float32
    )
    right_new[0] = stat_decay * right_old[0] + scale * right_prod


def make_stats(dp_index, strips, left_old, right_old):
    block_size = left_old.shape[-1]
    same = [jax.ShapeDtypeStruct(left_old.shape, jnp.float32)] * 2
    vmem = pl.BlockSpec(memory_space=pltpu.VMEM)
    return pl.pallas_call(
        functools.partial(stat_kernel, len(strips)),
        in_specs=[pl.BlockSpec(memory_space=pltpu.SMEM)] + [vmem] * (len(strips) + 2),
        out_specs=[vmem] * 2,
        out_shape=same,
        scratch_shapes=[pltpu.VMEM((block_size, block_size), jnp.bfloat16)],
        compiler_params=pltpu.CompilerParams(vmem_limit_bytes=vmem_bytes),
        cost_estimate=pl.CostEstimate(flops=1000, bytes_accessed=1000, transcendentals=0),
    )(dp_index.astype(jnp.int32)[None], *strips, left_old, right_old)


def on_device(grads, left_old, right_old, left_root, right_root):
    members, owners = lax.axis_size("dp"), lax.axis_size("blk")
    near = members // 2
    bits = near.bit_length() - 1
    block_size = left_root.shape[-1]
    strip_rows = left_old.shape[1]
    dp_index = lax.axis_index("dp")
    blk_index = lax.axis_index("blk")
    cols = grads.shape[3]
    spans = chunks_of(block_size)
    state = {}
    last = [None]

    def after(values):
        if last[0] is None:
            return values
        leaves, tree = jax.tree.flatten(values)
        leaves[0] = hold(leaves[0], jax.tree.leaves(last[0])[0])
        return jax.tree.unflatten(tree, leaves)

    def ways(given, k):
        way = given[k % len(given)]
        return [[j] for j in range(bits)][::way] if way else [list(range(bits))]

    def mask_of(group, which):
        return sum(1 << j for i, j in enumerate(group) if which >> i & 1)

    def pick_place(values, places, group, mask):
        rest = [p for p in places if not any(p >> j & 1 for j in group)]
        mine = sum(((dp_index ^ mask) >> j & 1) << i for i, j in enumerate(group))
        if len(rest) > 1 and len(group) == 1:
            inner = 1 << len([j for j in range(bits) if j < group[0] and any(p >> j & 1 for p in places)])
            shape = values.shape
            split = values.reshape(shape[0], len(places) // (2 * inner), 2, inner, *shape[2:])
            return pick(split, mine, 2).reshape(shape[0], len(rest), *shape[2:]), rest
        return lax.dynamic_slice_in_dim(values, mine, 1, 1), rest

    def chunk(k):
        start, stop = spans[k]
        return grads[0, :, start:stop].reshape(owners, near, (stop - start) // near, cols)

    def send_sum(k, values, places, group):
        sent, parts = [], []
        for which in range(1, 1 << len(group)):
            mask = mask_of(group, which)
            with jax.named_scope(f"R{group[0]}c{k}m{mask}"):
                part = pick_place(values, places, group, mask)[0].astype(jnp.bfloat16)
                sent.append(swap(part, "dp", mask))
                parts.append(part)
        return sent, parts

    def send_gather(k, strip, group):
        sent = []
        for which in range(1, 1 << len(group)):
            mask = mask_of(group, which)
            with jax.named_scope(f"A{group[0]}c{k}m{mask}"):
                sent.append(swap(strip, "dp", mask))
        return sent

    def first(k):
        places = list(range(near))
        group = ways(sum_ways, k)[0]
        state[k] = (chunk(k), places, send_sum(k, chunk(k), places, group)[0])

    def sum_step(k, s):
        sums = ways(sum_ways, k)
        if s < len(sums):
            values, places, received = state[k]
            received = after(received)
            own, places = pick_place(values, places, sums[s], 0)
            total = own.astype(jnp.float32)
            for piece in received:
                total = total + piece.astype(jnp.float32)
            if s + 1 < len(sums):
                sent, last[0] = send_sum(k, total, places, sums[s + 1])
                state[k] = (total, places, sent)
            else:
                total = total[:, 0]
                last[0] = total.astype(jnp.bfloat16)
                with jax.named_scope(f"Z{k}m0"):
                    state[k] = (total, swap(last[0], "dp", near))
        else:
            total, far = state[k]
            far = after(far)
            last[0] = (total + far.astype(jnp.float32)).astype(jnp.bfloat16)
            state[k] = last[0]

    def gather_step(g, s):
        gathers = ways(gather_ways, g)
        if s == 0:
            owned = [state[k] for k in groups[g]]
            owned = jnp.concatenate(owned, axis=1) if len(owned) > 1 else owned[0]
            if len(groups[g]) > 1:
                owned = after(owned)
            pieces = [pick(owned, blk_index, 0)]
            for m in range(1, owners):
                with jax.named_scope(f"B{g}m{m}"):
                    pieces.append(swap(pick(owned, blk_index ^ m, 0), "blk", m))
            state["g", g] = pieces
            if len(groups[g]) > 1:
                last[0] = owned
            return
        if s == 1:
            pieces = after(state["g", g])
            strip = jnp.concatenate(ordered(pieces, blk_index), axis=1)[None]
        else:
            strip, others = state["g", g]
            others = after(others)
            group = gathers[s - 2]
            mine = sum((dp_index >> j & 1) << i for i, j in enumerate(group))
            strip = jnp.concatenate(ordered([strip] + others, mine), axis=0)
        last[0] = strip
        if s - 1 < len(gathers):
            state["g", g] = (strip, send_gather(g, strip, gathers[s - 1]))
        else:
            state["g", g] = strip

    for k in range(len(spans)):
        first(k)
    for kind, index, stage in steps_of(bits):
        (sum_step if kind == "s" else gather_step)(index, stage)
    strips = []
    for g in range(len(groups)):
        places = [0]
        for group in ways(gather_ways, g):
            places = [p + mask_of(group, w) for w in range(1 << len(group)) for p in places]
        strip = state["g", g]
        if places != list(range(near)):
            strip = jnp.concatenate([strip[places.index(p)][None] for p in range(near)], axis=0)
        start = 0
        for k in groups[g]:
            depth = (spans[k][1] - spans[k][0]) // near
            strips.append(strip[:, start : start + depth].reshape(-1, block_size))
            start += depth

    aligned = cols % 128 == 0 and strip_rows % 128 == 0
    if aligned:
        back = list(make_update(blk_index, dp_index, strips, left_root, right_root, strip_rows, owners, cols))
    else:
        whole = jnp.concatenate(strips, axis=0)
        root_rows = lax.dynamic_slice_in_dim(left_root[0], dp_index * strip_rows, strip_rows, 0)
        half_done = jnp.dot(root_rows, whole, preferred_element_type=jnp.float32)
        full = jnp.dot(
            half_done.astype(jnp.bfloat16), right_root[0], preferred_element_type=jnp.float32
        )
        by_columns = full.astype(jnp.bfloat16).reshape(strip_rows, owners, cols)
        back = [pick(by_columns, blk_index ^ m, 1) for m in range(owners)]
    for m in range(1, owners):
        with jax.named_scope(f"U0m{m}"):
            back[m] = swap(back[m], "blk", m)
    if aligned:
        left_stat, right_stat = make_stats(dp_index, strips, left_old, right_old)
    else:
        own_rows = lax.dynamic_slice_in_dim(whole, dp_index * strip_rows, strip_rows, 0)
        own_columns = lax.dynamic_slice_in_dim(whole, dp_index * strip_rows, strip_rows, 1)
        left_prod = jnp.einsum("ik,jk->ij", own_rows, whole, preferred_element_type=jnp.float32)
        right_prod = jnp.einsum("ki,kj->ij", own_columns, whole, preferred_element_type=jnp.float32)
        stat_scale = (1.0 - stat_decay) / block_size
        left_stat = stat_decay * left_old + stat_scale * left_prod
        right_stat = stat_decay * right_old + stat_scale * right_prod
    update = jnp.stack(ordered(back, blk_index))
    return (update, left_stat, right_stat)


def solution(mesh):
    placed = (
        P("dp", None, None, "blk"),
        P("blk", "dp", None),
        P("blk", "dp", None),
        P("blk", None, None),
        P("blk", None, None),
    )
    return jax.shard_map(
        on_device,
        mesh=mesh,
        in_specs=placed,
        out_specs=(P(None, "dp", "blk"), P("blk", "dp", None), P("blk", "dp", None)),
        check_vma=False,
    )
```
